32 devices in a mesh: groups: 2 (over y), expert: 4 (over z), tensor: 4 (over x, core), sub: 1.
Axes of the slice: x: 2, y: 2, z: 4, core: 2. Of those that a mesh axis runs over, the one named last changes fastest.
Arguments:
- hidden_rows: bfloat16 [4, 320, 4096], P(None, ('groups', 'expert', 'tensor')), parts along dimension 1, may hold values from -6 to 6
- expert_ids: int32 [4, 320, 8], P(None, ('groups', 'expert', 'tensor')), parts along dimension 1, may hold values from 0 to 15, all different within a row; in each aligned block of 10 rows (0 to 9, 10 to 19, ..., all dimensions but the last counted through in order) at most 5 rows name the same one
- accepted: int32 [4, 64], P(None, ('groups', 'expert', 'tensor')), parts along dimension 1, may hold values from 0 to 4
- norm_gain: float32 [4096], replicated, may hold values from 0.5 to 1.5
- router: bfloat16 [4096, 16], replicated, may hold values from -0.0625 to 0.0625
- gate_weight: bfloat16 [16, 4096, 768], P(('expert', 'tensor'), None, 'sub'), may hold values from -0.09375 to 0.09375
- up_weight: bfloat16 [16, 4096, 768], P(('expert', 'tensor'), None, 'sub'), may hold values from -0.09375 to 0.09375
- down_weight: bfloat16 [16, 768, 4096], P(('expert', 'tensor'), 'sub'), may hold values from -0.21875 to 0.21875
- draft_gain: float32 [4096], replicated, may hold values from 0.5 to 1.5
- draft_gate: bfloat16 [4096, 6144], P(None, ('expert', 'tensor')), may hold values from -0.09375 to 0.09375
- draft_up: bfloat16 [4096, 6144], P(None, ('expert', 'tensor')), may hold values from -0.09375 to 0.09375
- draft_down: bfloat16 [6144, 4096], P(('expert', 'tensor')), may hold values from -0.078125 to 0.078125
- final_gain: float32 [4096], replicated, may hold values from 0.5 to 1.5
Outputs:
- verified: bfloat16 [4, 320, 4096], P(None, ('groups', 'expert', 'tensor')), parts along dimension 1
- draft_out: bfloat16 [4, 64, 4096], P(None, ('groups', 'expert', 'tensor')), parts along dimension 1
The draws below stay inside these ranges and needn't reach their ends.
There are 2 independent parts, one for each index of `groups`. The reference program is written for one: setup_inputs(seed, part) draws one part's arguments, and reference() takes and returns one part's arrays. A program takes and returns all parts, laid end to end along the dimension named above; an argument that names none is the same for every part. Nothing has to cross between parts.
Inputs may be any that keep to these rules, and one draw needn't show every extreme that they name: `expert_ids`: the 8 ids of a row differ. In each aligned block of 10 rows no expert is named by more than 5 rows, and in some block one expert is named by exactly 5 rows.
All inputs are finite; a program needn't handle non-finite values.
Results may differ from the reference program's by a relative error of at most 0.0068.
Values may be sent and summed in bfloat16 or wider, within the bound.
No kernel may reach another device: no remote copies, remote signals or barrier semaphores. Data moves between devices by JAX's collectives and lax.ppermute only.
A program may use at most 128 MiB of HBM per device.

```python
import math
import jax
import jax.numpy as jnp
import numpy as np
from jax import lax

D = 4096
MOE_FF = 768
DFF = 6144
TOP = 8
DRAFT = 5
ROUNDS = 4
SPLIT = 1
FF_DEV = 768
EXPERTS = 16
ROWS_DEV = 10
ROWS = 160
REQS = 32
CAP = 5


def set_ends(drawn, stream_key, low, high):
    place = [jax.random.randint(jax.random.fold_in(stream_key, axis), (), 0, length) for axis, length in enumerate(drawn.shape)]
    main_axis = drawn.shape.index(max(drawn.shape))
    next_to = place[:main_axis] + [(place[main_axis] + 1) % drawn.shape[main_axis]] + place[main_axis + 1:]
    return drawn.at[tuple(place)].set(low).at[tuple(next_to)].set(high)


def levels(stream_key, dims, pieces, smallest, high):
    def one(axis_at, shards_of):
        draws = jax.random.uniform(jax.random.fold_in(jax.random.fold_in(stream_key, 6), axis_at), (shards_of,), jnp.float32, smallest / len(pieces), high / len(pieces))
        return jnp.repeat(jnp.exp(draws), dims[axis_at] // shards_of).reshape((-1,) + (1,) * (len(dims) - axis_at - 1))

    factor_of = one(*pieces[0])
    for cut in pieces[1:]:
        factor_of = factor_of * one(*cut)
    return factor_of


def routed_block(key, own, number, rows, count, top, bound, slope):
    ranking = jax.random.permutation(key, count)
    crowded, ordinary = shares(count, rows * top, bound, slope, True), shares(count, rows * top, bound, slope, False)
    places = jnp.arange(count)

    def named(lengths, rotation):
        used = int((lengths > 0).sum())
        fixed = max(1, used // 4)
        moved = fixed + (places - fixed + rotation * (used - fixed)) % max(1, count - fixed)
        return jnp.zeros((count,), jnp.int32).at[ranking[jnp.where(places < fixed, places, moved)]].set(jnp.asarray(lengths, jnp.int32))

    lengths = jnp.where(number % 4 == 0, named(crowded, number // 4), named(ordinary, number - number // 4 - 1))
    mixed = jax.random.permutation(jax.random.fold_in(own, 3), count)
    source_of, sink = mixed[0:count // 2 * 2:2], mixed[1:count // 2 * 2:2]
    margin = jnp.minimum(lengths[source_of] - 1, bound - lengths[sink]) // 2
    margin = jnp.where((source_of == ranking[0]) | (sink == ranking[0]) | (lengths[sink] == 0), 0, jnp.maximum(margin, 0))
    moved = jax.random.randint(jax.random.fold_in(own, 4), (count // 2,), 0, 1 << 20) % (margin + 1)
    lengths = lengths.at[source_of].add(-moved).at[sink].add(moved)
    members = jnp.searchsorted(jnp.cumsum(lengths), jnp.arange(rows * top), side="right").astype(jnp.int32)
    listing = members.reshape(top, rows).T
    listing = listing[jax.random.permutation(jax.random.fold_in(own, 1), rows)]
    rotation = jax.random.randint(jax.random.fold_in(own, 2), (rows, 1), 0, top)
    return jnp.take_along_axis(listing, (jnp.arange(top)[None, :] + rotation) % top, axis=1)


def shares(count, total, limit, slope, full):
    loads = [(1 << 20) // math.isqrt(grade ** slope) + 1 for grade in range(1, count + 1)]
    largest = limit if full else min(limit, max(-(-total // count), total * loads[0] // sum(loads)))
    least = 1 if total - largest >= count - 1 else 0
    holding, rest = [largest] + [least] * (count - 1), total - largest - least * (count - 1)
    while rest > 0:
        movable = [i for i in range(1, count) if holding[i] < largest] or [i for i in range(1, count) if holding[i] < limit]
        mass, budget = sum([loads[i] for i in movable]), rest
        for i in movable:
            addition = min(limit - holding[i], max(1, budget * loads[i] // mass), rest)
            holding[i] = holding[i] + addition
            rest = rest - addition
    return np.array(holding)


def scatter_about(stream_key, shape, width, reach, shards=(), kind=jnp.bfloat16):
    level = levels(stream_key, shape, shards, -0.22, 0.18) if shards else 1.0
    values = jax.random.normal(stream_key, shape, jnp.float32) * width * level
    return jnp.minimum(jnp.maximum(values, -reach), reach).astype(kind)


def setup_inputs(seed: int = 0, part: int = 0) -> dict:
    keys = jax.random.split(jax.random.key(seed), 14)
    own_keys = jax.random.split(jax.random.fold_in(keys[13], part), 14)
    hidden_rows = scatter_about(own_keys[0], (ROUNDS, ROWS, D), 1.0, 6.0, ((1, 16),))
    expert_ids_keys = jax.random.split(jax.random.fold_in(own_keys[1], 1), ROUNDS * ROWS // ROWS_DEV)
    expert_ids_turns = jax.random.permutation(jax.random.fold_in(own_keys[1], 3), ROUNDS * ROWS // ROWS_DEV)
    expert_ids = jax.vmap(lambda own, number: routed_block(jax.random.fold_in(own_keys[1], 2), own, number, ROWS_DEV, EXPERTS, TOP, CAP, 2))(expert_ids_keys, expert_ids_turns).reshape((ROUNDS, ROWS, TOP))
    accepted = set_ends(jax.random.randint(own_keys[2], (ROUNDS, REQS), 0, DRAFT), jax.random.fold_in(own_keys[2], 1), 0, DRAFT - 1).astype(jnp.int32)
    norm_gain = jnp.clip(1.0 + 0.1 * jax.random.normal(keys[3], (D,), jnp.float32), 0.5, 1.5)
    router = scatter_about(keys[4], (D, EXPERTS), (2 * D) ** -0.5, 0.0625)
    gate_weight = scatter_about(keys[5], (EXPERTS, D, MOE_FF), D ** -0.5, 0.09375, ((0, 16),))
    up_weight = scatter_about(keys[6], (EXPERTS, D, MOE_FF), D ** -0.5, 0.09375, ((0, 16),))
    down_weight = scatter_about(keys[7], (EXPERTS, MOE_FF, D), MOE_FF ** -0.5, 0.21875, ((0, 16),))
    draft_gain = jnp.clip(1.0 + 0.1 * jax.random.normal(keys[8], (D,), jnp.float32), 0.5, 1.5)
    draft_gate = scatter_about(keys[9], (D, DFF), D ** -0.5, 0.09375, ((1, 16),))
    draft_up = scatter_about(keys[10], (D, DFF), D ** -0.5, 0.09375, ((1, 16),))
    draft_down = scatter_about(keys[11], (DFF, D), DFF ** -0.5, 0.078125, ((0, 16),))
    final_gain = jnp.clip(1.0 + 0.1 * jax.random.normal(keys[12], (D,), jnp.float32), 0.5, 1.5)
    return dict(hidden_rows=hidden_rows, expert_ids=expert_ids, accepted=accepted, norm_gain=norm_gain, router=router, gate_weight=gate_weight, up_weight=up_weight, down_weight=down_weight, draft_gain=draft_gain, draft_gate=draft_gate, draft_up=draft_up, draft_down=draft_down, final_gain=final_gain)


EPSILON = 1e-06

def rms_scale(values, weights):
    values = values.astype(jnp.float32)
    mean_square = lax.optimization_barrier(jnp.mean(values * values, axis=-1, keepdims=True))
    return values * lax.rsqrt(mean_square + EPSILON) * weights

def slot_positions(chosen_ids):
    blocks = chosen_ids.reshape(ROWS // ROWS_DEV, ROWS_DEV * TOP)
    one_hot = (blocks[:, :, None] == jnp.arange(EXPERTS, dtype=jnp.int32)[None, None, :]).astype(jnp.int32)
    rank_values = jnp.cumsum(one_hot, axis=1) - 1
    positions = lax.optimization_barrier(jnp.sum(rank_values * one_hot, axis=2))
    return positions.reshape(ROWS, TOP).astype(jnp.int32)

def expert_apply(operands):
    inputs, gate_matrix, up_matrix, down_matrix = operands
    gate_values = jnp.dot(inputs, gate_matrix, preferred_element_type=jnp.float32)
    up_values = jnp.dot(inputs, up_matrix, preferred_element_type=jnp.float32)
    active = (jax.nn.silu(gate_values) * up_values).astype(jnp.bfloat16)
    summed_out = jnp.zeros((inputs.shape[0], D), jnp.float32)
    for group_index in range(SPLIT):
        lower = group_index * FF_DEV
        part_sum = jnp.dot(active[:, lower:lower + FF_DEV], down_matrix[lower:lower + FF_DEV], preferred_element_type=jnp.float32)
        summed_out = summed_out + lax.optimization_barrier(part_sum.astype(jnp.bfloat16)).astype(jnp.float32)
    return summed_out.astype(jnp.bfloat16)

def reference(hidden_rows, expert_ids, accepted, norm_gain, router, gate_weight, up_weight, down_weight, draft_gain, draft_gate, draft_up, draft_down, final_gain):
    block_total = ROWS // ROWS_DEV
    total_slots = EXPERTS * block_total * CAP
    verified_list = []
    draft_list = []
    for round_index in range(ROUNDS):
        rows = hidden_rows[round_index]
        chosen_ids = expert_ids[round_index].astype(jnp.int32)
        normed = rms_scale(rows, norm_gain).astype(jnp.bfloat16)
        logits = jnp.dot(normed, router, preferred_element_type=jnp.float32)
        chosen = jnp.take_along_axis(logits, chosen_ids, axis=1)
        exp_values = jnp.exp(chosen)
        gate_share = exp_values / lax.optimization_barrier(jnp.sum(exp_values, axis=1, keepdims=True))
        positions = slot_positions(chosen_ids)
        block_index = (jnp.arange(ROWS, dtype=jnp.int32) // ROWS_DEV)[:, None]
        slot_index = ((chosen_ids * block_total + block_index) * CAP + positions).astype(jnp.int32)
        row_ids = jnp.broadcast_to(jnp.arange(ROWS, dtype=jnp.int32)[:, None], (ROWS, TOP))
        slot_rows = jnp.full((total_slots,), ROWS, jnp.int32).at[slot_index.reshape(-1)].set(row_ids.reshape(-1))
        padded = jnp.concatenate([normed, jnp.zeros((1, D), normed.dtype)], axis=0)
        buffers = padded[slot_rows].reshape(EXPERTS, block_total * CAP, D)
        outputs = lax.map(expert_apply, (buffers, gate_weight, up_weight, down_weight)).reshape(total_slots, D)
        picked = outputs[slot_index].astype(jnp.float32)
        mixed_rows = rows.astype(jnp.float32) + lax.optimization_barrier(jnp.sum(gate_share[:, :, None] * picked, axis=1))
        verified = mixed_rows.astype(jnp.bfloat16)
        chosen_rows = (jnp.arange(REQS, dtype=jnp.int32) * DRAFT + accepted[round_index].astype(jnp.int32)).astype(jnp.int32)
        features = verified[chosen_rows]
        draft_in = rms_scale(features, draft_gain).astype(jnp.bfloat16)
        hidden = (jax.nn.silu(jnp.dot(draft_in, draft_gate, preferred_element_type=jnp.float32)) * jnp.dot(draft_in, draft_up, preferred_element_type=jnp.float32)).astype(jnp.bfloat16)
        summed = features.astype(jnp.float32) + jnp.dot(hidden, draft_down, preferred_element_type=jnp.float32)
        draft_out = rms_scale(summed, final_gain).astype(jnp.bfloat16)
        verified_list.append(verified)
        draft_list.append(draft_out)
    return (jnp.stack(verified_list, axis=0), jnp.stack(draft_list, axis=0))
```

```python
import functools

import jax
import jax.numpy as jnp
from jax import lax
from jax.experimental import pallas as pl
from jax.experimental.pallas import tpu as pltpu
from jax.sharding import PartitionSpec as P

EPSILON = 1e-06
BF = jnp.bfloat16
F32 = jnp.float32
LANES = 128
VMEM_LIMIT = 48 * 1024 * 1024


def fdot(a, b):
    return jnp.dot(a, b, preferred_element_type=F32)


def iota(shape, axis):
    return lax.broadcasted_iota(jnp.int32, shape, axis)


def accepted_column(accepted_ref, size, axis, per_round, chunk):
    shape = (size, 1) if axis == 0 else (1, size)
    request = lax.rem(iota(shape, axis), chunk)
    found = jnp.zeros(shape, jnp.int32)
    for number in range(chunk):
        value = accepted_ref[number // per_round, number % per_round]
        found = jnp.where(request == number, value, found)
    return found


def sources(accepted_ref, size, axis, per_round, chunk, draft):
    shape = (size, 1) if axis == 0 else (1, size)
    place = iota(shape, axis)
    request = lax.rem(place, chunk)
    layer = lax.div(place, chunk)
    wanted = accepted_column(accepted_ref, size, axis, per_round, chunk)
    other = layer - 1
    inside = jnp.where(layer == 0, wanted, other + (other >= wanted).astype(jnp.int32))
    return lax.div(request, per_round), lax.rem(request, per_round) * draft + inside


def prep_kernel(sizes, accepted_ref, hidden_ref, ids_ref, gain_ref, router_ref, *outs):
    rounds, rows, experts, top, per_round, draft = sizes
    chunk = rounds * per_round
    total = rounds * rows
    width = hidden_ref.shape[2]
    ext_refs, hid_refs = outs[: len(outs) // 2], outs[len(outs) // 2 :]
    source_round, source_row = sources(accepted_ref, total, 0, per_round, chunk, draft)
    lane = iota((rows, LANES), 1)
    moved = None
    for number in range(rounds):
        raw = hidden_ref[number]
        values = raw.astype(F32)
        mean_square = jnp.mean(values * values, axis=-1, keepdims=True)
        normed = (values * lax.rsqrt(mean_square + EPSILON) * gain_ref[...]).astype(BF)
        logits = fdot(normed, router_ref[...])
        ids = ids_ref[number]
        expert = iota((rows, experts), 1)
        named = ids[:, 0:1] == expert
        for k in range(1, top):
            named = named | (ids[:, k : k + 1] == expert)
        powers = jnp.where(named, jnp.exp(logits), 0.0)
        share = powers / jnp.sum(powers, axis=1, keepdims=True)
        high = share.astype(BF)
        rest = (share - high.astype(F32)).astype(BF)
        place = (
            (source_round == number) & (source_row == iota((total, rows), 1))
        ).astype(BF)
        parts = [fdot(place, normed), fdot(place, raw), fdot(place, high), fdot(place, rest)]
        moved = parts if moved is None else [a + b for a, b in zip(moved, parts)]
    normed, raw, high, rest = [part.astype(BF) for part in moved]
    pad = jnp.zeros((total, LANES - 2 * experts), BF)
    tail = jnp.concatenate([high, rest] + ([pad] if 2 * experts < LANES else []), axis=1)
    first = 0
    for ext_ref, hid_ref in zip(ext_refs, hid_refs):
        count = ext_ref.shape[0]
        ext_ref[:, :width] = normed[first : first + count]
        ext_ref[:, width:] = tail[first : first + count]
        hid_ref[...] = raw[first : first + count]
        first += count


def prep(hidden, ids, accepted, gain, router, counts):
    rounds, rows, width = hidden.shape
    sizes = (rounds, rows, router.shape[1], ids.shape[2], accepted.shape[1], rows // accepted.shape[1])
    vmem = pl.BlockSpec(memory_space=pltpu.VMEM)
    return pl.pallas_call(
        functools.partial(prep_kernel, sizes),
        out_shape=[jax.ShapeDtypeStruct((count, width + LANES), BF) for count in counts]
        + [jax.ShapeDtypeStruct((count, width), BF) for count in counts],
        in_specs=[pl.BlockSpec(memory_space=pltpu.SMEM)] + [vmem] * 4,
        out_specs=[vmem] * (2 * len(counts)),
        compiler_params=pltpu.CompilerParams(vmem_limit_bytes=VMEM_LIMIT),
        name="prep",
    )(accepted, hidden, ids, gain.reshape(1, width), router)


def unit_kernel(gated, steps, mark_ref, x_ref, gate_ref, up_ref, down_ref, out_ref, acc_ref):
    step = pl.program_id(1)
    width = out_ref.shape[1]
    x = x_ref[:, :width]
    gate = fdot(x, gate_ref[...])
    up = fdot(x, up_ref[...])
    active = (gate / (1.0 + jnp.exp(-gate)) * up).astype(BF)
    term = fdot(active, down_ref[...])

    @pl.when(step == 0)
    def _():
        acc_ref[...] = term

    @pl.when(step > 0)
    def _():
        acc_ref[...] += term

    @pl.when(step == steps - 1)
    def _():
        total = acc_ref[...]
        if gated:
            share = jnp.sum(x_ref[:, width:].astype(F32) * mark_ref[...], axis=1, keepdims=True)
            total = total * share
        out_ref[...] = total.astype(BF)


def units(x, mark, gate, up, down, gated, tile):
    count, columns = x.shape
    hidden, width = down.shape
    rows = min(count, 256)
    tile = min(tile, hidden)
    if hidden % tile:
        tile = hidden
    steps = hidden // tile
    return pl.pallas_call(
        functools.partial(unit_kernel, gated, steps),
        grid=(count // rows, steps),
        out_shape=jax.ShapeDtypeStruct((count, width), BF),
        in_specs=[
            pl.BlockSpec((1, LANES), lambda m, f: (0, 0)),
            pl.BlockSpec((rows, columns), lambda m, f: (m, 0)),
            pl.BlockSpec((width, tile), lambda m, f: (0, f)),
            pl.BlockSpec((width, tile), lambda m, f: (0, f)),
            pl.BlockSpec((tile, width), lambda m, f: (f, 0)),
        ],
        out_specs=pl.BlockSpec((rows, width), lambda m, f: (m, 0)),
        scratch_shapes=[pltpu.VMEM((rows, width), F32)],
        compiler_params=pltpu.CompilerParams(vmem_limit_bytes=VMEM_LIMIT),
        cost_estimate=pl.CostEstimate(
            flops=6 * count * hidden * width,
            bytes_accessed=2 * (3 * hidden * width + 2 * count * width),
            transcendentals=count * hidden,
        ),
        name="experts" if gated else "drafter",
    )(mark, x, gate, up, down)


def mid_kernel(hid_ref, gain_ref, *refs):
    verified_ref, draft_ref = refs[-2:]
    total = hid_ref[...].astype(F32) + sum(ref[...].astype(F32) for ref in refs[:-2])
    verified = total.astype(BF)
    verified_ref[...] = verified
    values = verified.astype(F32)
    mean_square = jnp.mean(values * values, axis=-1, keepdims=True)
    draft_ref[...] = (values * lax.rsqrt(mean_square + EPSILON) * gain_ref[...]).astype(BF)


def mid(hid, parts, gain):
    return pl.pallas_call(
        mid_kernel,
        out_shape=[jax.ShapeDtypeStruct(hid.shape, BF)] * 2,
        compiler_params=pltpu.CompilerParams(vmem_limit_bytes=VMEM_LIMIT),
        name="accepted_norm",
    )(hid, gain.reshape(1, -1), *parts)


def last_kernel(hid_ref, gain_ref, *refs):
    out_ref = refs[-1]
    total = hid_ref[...].astype(F32) + sum(ref[...].astype(F32) for ref in refs[:-1])
    mean_square = jnp.mean(total * total, axis=-1, keepdims=True)
    out_ref[...] = (total * lax.rsqrt(mean_square + EPSILON) * gain_ref[...]).astype(BF)


def last(hid, parts, gain):
    return pl.pallas_call(
        last_kernel,
        out_shape=jax.ShapeDtypeStruct(hid.shape, BF),
        compiler_params=pltpu.CompilerParams(vmem_limit_bytes=VMEM_LIMIT),
        name="draft_norm",
    )(hid, gain.reshape(1, -1), *parts)


def merge_kernel(sizes, groups, accepted_ref, *refs):
    rounds, rows, per_round, draft = sizes
    chunk = rounds * per_round
    out_ref = refs[-1]
    pieces = []
    first = 0
    for group in groups:
        members = refs[first : first + group]
        first += group
        if group == 1:
            pieces.append(members[0][...])
        else:
            pieces.append(sum(ref[...].astype(F32) for ref in members).astype(BF))
    total = rounds * rows
    source_round, source_row = sources(accepted_ref, total, 1, per_round, chunk, draft)
    for number in range(rounds):
        place = (
            (source_round == number) & (source_row == iota((rows, total), 0))
        ).astype(BF)
        result = None
        first = 0
        for piece in pieces:
            count = piece.shape[0]
            term = fdot(place[:, first : first + count], piece)
            result = term if result is None else result + term
            first += count
        out_ref[number] = result.astype(BF)


def merge(accepted, groups, shape, draft):
    rounds, rows, width = shape
    sizes = (rounds, rows, accepted.shape[1], draft)
    vmem = pl.BlockSpec(memory_space=pltpu.VMEM)
    flat = [array for group in groups for array in group]
    return pl.pallas_call(
        functools.partial(merge_kernel, sizes, [len(group) for group in groups]),
        out_shape=jax.ShapeDtypeStruct(shape, BF),
        in_specs=[pl.BlockSpec(memory_space=pltpu.SMEM)] + [vmem] * len(flat),
        out_specs=vmem,
        compiler_params=pltpu.CompilerParams(vmem_limit_bytes=VMEM_LIMIT),
        name="merge",
    )(accepted, *flat)


class Links:
    def __init__(self, lines, columns):
        self.lines = lines
        self.columns = columns

    def line(self, x, shift):
        n = self.lines
        return lax.ppermute(x, "expert", [(i, (i + shift) % n) for i in range(n)])

    def cross(self, x, bit):
        return lax.ppermute(x, "tensor", [(i, i ^ bit) for i in range(self.columns)])

    def gather(self, x):
        blocks = [x] + [self.line(x, shift) for shift in range(1, self.lines)]
        bit = self.columns // 2
        while bit > 1:
            blocks = blocks + [self.cross(block, bit) for block in blocks]
            bit //= 2
        whole = jnp.concatenate(blocks, axis=0)
        if bit == 1:
            whole = jnp.concatenate([whole, self.cross(whole, 1)], axis=0)
        return whole

    def scatter(self, whole):
        bit = 1
        while bit < self.columns:
            half = whole.shape[0] // 2
            keep, send = whole[:half], whole[half:]
            whole = (keep.astype(F32) + self.cross(send, bit).astype(F32)).astype(BF)
            bit *= 2
        size = whole.shape[0] // self.lines
        terms = [whole[:size]]
        for shift in range(1, self.lines):
            block = whole[shift * size : (shift + 1) * size]
            terms.append(self.line(block, -shift))
        return terms


def local(
    lines,
    columns,
    subs,
    hidden_rows,
    expert_ids,
    accepted,
    norm_gain,
    router,
    gate_weight,
    up_weight,
    down_weight,
    draft_gain,
    draft_gate,
    draft_up,
    draft_down,
    final_gain,
):
    rounds, rows, width = hidden_rows.shape
    experts = router.shape[1]
    requests = accepted.shape[1]
    draft = rows // requests
    chunk = rounds * requests
    links = Links(lines, columns)
    me = lax.axis_index("expert") * columns + lax.axis_index("tensor")
    lane = jnp.arange(LANES, dtype=jnp.int32)[None, :]
    mark = ((lane == me) | (lane == me + experts)).astype(F32)
    others = rounds * rows - chunk
    counts = [chunk, others // 2, others - others // 2]
    outs = prep(hidden_rows, expert_ids, accepted, norm_gain, router, counts)
    exts, hids = outs[:3], outs[3:]

    def routed(ext):
        whole = links.gather(ext)
        out = units(whole, mark, gate_weight[0], up_weight[0], down_weight[0], True, 256)
        terms = links.scatter(out)
        if subs > 1:
            total = sum(term.astype(F32) for term in terms)
            terms = [lax.psum(total, "sub")]
        return terms

    first = routed(exts[0])
    features, draft_in = mid(hids[0], first, draft_gain)
    second = routed(exts[1])
    whole = links.gather(draft_in)
    out = units(whole, mark, draft_gate, draft_up, draft_down, False, 128)
    third = routed(exts[2])
    draft_out = last(features, links.scatter(out), final_gain)
    verified = merge(
        accepted,
        [[features], [hids[1]] + second, [hids[2]] + third],
        hidden_rows.shape,
        draft,
    )
    return verified, draft_out.reshape(rounds, requests, width)


def solution(mesh):
    placed = (
        P(None, ("groups", "expert", "tensor"), None),
        P(None, ("groups", "expert", "tensor"), None),
        P(None, ("groups", "expert", "tensor")),
        P(),
        P(),
        P(("expert", "tensor"), None, "sub"),
        P(("expert", "tensor"), None, "sub"),
        P(("expert", "tensor"), "sub", None),
        P(),
        P(None, ("expert", "tensor")),
        P(None, ("expert", "tensor")),
        P(("expert", "tensor"), None),
        P(),
    )
    body = functools.partial(
        local, mesh.shape["expert"], mesh.shape["tensor"], mesh.shape["sub"]
    )
    return jax.shard_map(
        body,
        mesh=mesh,
        in_specs=placed,
        out_specs=(
            P(None, ("groups", "expert", "tensor"), None),
            P(None, ("groups", "expert", "tensor"), None),
        ),
        check_vma=False,
    )
```

```python
import functools

import jax
import jax.numpy as jnp
from jax import lax
from jax.experimental import pallas as pl
from jax.experimental.pallas import tpu as pltpu
from jax.sharding import PartitionSpec as P

EPSILON = 1e-06
BF = jnp.bfloat16
F32 = jnp.float32
LANES = 128
MIB = 1024 * 1024
SMALL = pltpu.CompilerParams(vmem_limit_bytes=16 * MIB)
BLOCK_ROWS = 256
CUT = 2
ANYWHERE = pl.BlockSpec(memory_space=pl.ANY)
HBM = pl.BlockSpec(memory_space=pltpu.HBM)
SCALARS = pl.BlockSpec(memory_space=pltpu.SMEM)
VECTORS = pl.BlockSpec(memory_space=pltpu.VMEM)


def fdot(a, b):
    return jnp.dot(a, b, preferred_element_type=F32)


def fdot_t(a, b):
    return lax.dot_general(a, b, (((1,), (1,)), ((), ())), preferred_element_type=F32)


def iota(shape, axis):
    return lax.broadcasted_iota(jnp.int32, shape, axis)


def rms(values):
    return values * lax.rsqrt(jnp.mean(values * values, axis=-1, keepdims=True) + EPSILON)


def struct(rows, columns):
    return jax.ShapeDtypeStruct((rows, columns), BF)


def accepted_vector(accepted_ref, request, rounds):
    place = iota((rounds, 1), 0)
    found = jnp.zeros((rounds, 1), jnp.int32)
    for number in range(rounds):
        found = jnp.where(place == number, accepted_ref[request, number], found)
    return found


def reorder(layers, accepted_ref, hidden_ref, ids_ref, gain_ref, router_ref, ext_ref, hid_ref):
    rows, rounds, width = hidden_ref.shape
    requests = accepted_ref.shape[0]
    draft = rows // requests
    top, experts = ids_ref.shape[1], router_ref.shape[0]
    chunk = rounds * requests
    taken = [accepted_vector(accepted_ref, request, rounds) for request in range(requests)]
    pieces = []
    for layer in layers:
        for request in range(requests):
            first = request * draft
            if layer == 0:
                found = hidden_ref[first].astype(F32)
                for inside in range(1, draft):
                    found = jnp.where(
                        taken[request] == inside, hidden_ref[first + inside].astype(F32), found
                    )
            else:
                found = jnp.where(
                    taken[request] >= layer,
                    hidden_ref[first + layer - 1].astype(F32),
                    hidden_ref[first + layer].astype(F32),
                )
            pieces.append(found)
    raw = jnp.concatenate(pieces, axis=0)
    hid_ref[...] = raw.astype(BF)
    normed = (rms(raw) * gain_ref[...]).astype(BF)
    ext_ref[:, :width] = normed
    count = len(layers) * chunk
    logits = fdot_t(normed, router_ref[...])
    place = iota((count, rows), 0)
    source = iota((count, rows), 1)
    wanted = jnp.full((count, rows), -1, jnp.int32)
    for number, layer in enumerate(layers):
        for request in range(requests):
            for turn in range(rounds):
                value = accepted_ref[request, turn]
                if layer > 0:
                    value = jnp.where(value >= layer, layer - 1, layer)
                row = number * chunk + request * rounds + turn
                wanted = jnp.where(place == row, value + request * draft, wanted)
    chosen = wanted == source
    named = None
    for turn in range(rounds):
        ids = ids_ref[turn]
        expert = iota((experts, rows), 0)
        hot = ids[0:1] == expert
        for k in range(1, top):
            hot = hot | (ids[k : k + 1] == expert)
        pick = (chosen & (lax.rem(place, rounds) == turn)).astype(F32).astype(BF)
        term = fdot_t(pick, hot.astype(F32).astype(BF))
        named = term if named is None else named + term
    powers = jnp.where(named > 0.5, jnp.exp(logits), 0.0)
    share = powers / jnp.sum(powers, axis=1, keepdims=True)
    high = share.astype(BF).astype(F32)
    tail = [high, share - high]
    if 2 * experts < LANES:
        tail.append(jnp.zeros((count, LANES - 2 * experts), F32))
    ext_ref[:, width:] = jnp.concatenate(tail, axis=1).astype(BF)


def prep_kernel(groups, columns, experts, *refs):
    sources, outs, targets, sems = refs[:5], refs[5:-6], refs[-6:-1], refs[-1]
    moves = [
        pltpu.make_async_copy(source, target, sems.at[number])
        for number, (source, target) in enumerate(zip(sources, targets))
    ]
    for move in moves:
        move.start()
    me = lax.axis_index("expert") * columns + lax.axis_index("tensor")
    lane = iota((1, LANES), 1)
    outs[-1][...] = ((lane == me) | (lane == me + experts)).astype(F32)
    for move in moves:
        move.wait()
    for number, layers in enumerate(groups):
        reorder(layers, *targets, outs[2 * number], outs[2 * number + 1])


def prep(inputs, groups, columns):
    accepted, hidden = inputs[:2]
    rows, rounds, width = hidden.shape
    shapes = []
    for layers in groups:
        count = len(layers) * rounds * accepted.shape[0]
        shapes += [struct(count, width + LANES), struct(count, width)]
    shapes.append(jax.ShapeDtypeStruct((1, LANES), F32))
    return pl.pallas_call(
        functools.partial(prep_kernel, groups, columns, inputs[-1].shape[0]),
        out_shape=shapes,
        in_specs=[HBM] * 5,
        out_specs=[VECTORS] * len(shapes),
        scratch_shapes=[pltpu.SMEM(accepted.shape, jnp.int32)]
        + [pltpu.VMEM(array.shape, array.dtype) for array in inputs[1:]]
        + [pltpu.SemaphoreType.DMA((5,))],
        compiler_params=pltpu.CompilerParams(vmem_limit_bytes=56 * MIB),
        name="prep",
    )(*inputs)


def hold(arrays, after):
    held = pl.pallas_call(
        lambda *refs: None,
        out_shape=[struct(*array.shape) for array in arrays],
        in_specs=[ANYWHERE] * (len(arrays) + len(after)),
        out_specs=[ANYWHERE] * len(arrays),
        input_output_aliases={number: number for number in range(len(arrays))},
        compiler_params=SMALL,
        name="hold",
    )(*arrays, *after)
    return list(held)


def pack_kernel(count, cut, *refs):
    whole = jnp.concatenate([ref[...] for ref in refs[:count]], axis=0)
    rows = whole.shape[0] // cut
    for number, out_ref in enumerate(refs[-cut:]):
        out_ref[...] = whole[number * rows : (number + 1) * rows]


def pack(blocks, after, cut=1):
    rows, width = sum(block.shape[0] for block in blocks), blocks[0].shape[1]
    outs = pl.pallas_call(
        functools.partial(pack_kernel, len(blocks), cut),
        out_shape=[struct(rows // cut, width)] * cut,
        in_specs=[VECTORS] * len(blocks) + [ANYWHERE] * len(after),
        out_specs=[VECTORS] * cut,
        compiler_params=SMALL,
        name="pack",
    )(*blocks, *after)
    return outs[0] if cut == 1 else list(outs)


def cut_kernel(count, first, rows, *refs):
    blocks = [ref[...] for ref in refs[:count]]
    refs[-1][...] = jnp.concatenate([block[first : first + rows] for block in blocks], axis=0)


def cut(blocks, first, rows, after, near=()):
    width = blocks[0].shape[1]
    count = len(blocks)
    return pl.pallas_call(
        functools.partial(cut_kernel, count, first, rows),
        out_shape=struct(count * rows, width),
        in_specs=[VECTORS] * count + [ANYWHERE] * len(after) + [VECTORS] * len(near),
        out_specs=VECTORS,
        compiler_params=SMALL,
        name="cut",
    )(*blocks, *after, *near)


def add_kernel(*refs):
    refs[-1][...] = sum(ref[...].astype(F32) for ref in refs[:-1]).astype(BF)


def add(arrays):
    return pl.pallas_call(
        add_kernel,
        out_shape=struct(*arrays[0].shape),
        compiler_params=SMALL,
        name="add",
    )(*arrays)


def fold_kernel(comes, parts, keep_ref, *refs):
    come_refs, out_refs = refs[:comes], refs[-parts:]
    rows = out_refs[0].shape[0]
    come = jnp.concatenate([ref[...] for ref in come_refs], axis=0).astype(F32)
    total = keep_ref[...].astype(F32) + come
    for number, out_ref in enumerate(out_refs):
        out_ref[...] = total[number * rows : (number + 1) * rows].astype(BF)


def fold(keep, comes, parts, after):
    rows, width = keep.shape
    return pl.pallas_call(
        functools.partial(fold_kernel, len(comes), parts),
        out_shape=[struct(rows // parts, width)] * parts,
        in_specs=[VECTORS] * (1 + len(comes)) + [ANYWHERE] * len(after),
        out_specs=[VECTORS] * parts,
        compiler_params=SMALL,
        name="fold",
    )(keep, *comes, *after)


def unit_kernel(gated, parts, group, mark_ref, *refs):
    x_refs, (gate_ref, up_ref, down_ref) = refs[:parts], refs[parts : parts + 3]
    out_refs, (all_ref, active_ref) = refs[-parts - 2 : -2], refs[-2:]
    rows, width = out_refs[0].shape
    hidden = gate_ref.shape[1]
    tile = min(256, hidden)
    columns = min(512, width)
    for first in range(0, parts, group):
        members = list(range(first, min(first + group, parts)))
        count = len(members) * rows
        for place, number in enumerate(members):
            all_ref[place * rows : (place + 1) * rows] = x_refs[number][:, :width]

        for step in range(0, hidden, tile):
            at = slice(step, step + tile)
            gate = fdot(all_ref[:count], gate_ref[:, at])
            up = fdot(all_ref[:count], up_ref[:, at])
            active_ref[:count, at] = (gate / (1.0 + jnp.exp(-gate)) * up).astype(BF)

        share = None
        if gated:
            tail = jnp.concatenate([x_refs[number][:, width:] for number in members], axis=0)
            share = jnp.sum(tail.astype(F32) * mark_ref[...], axis=1, keepdims=True)

        for step in range(0, width, columns):
            at = slice(step, step + columns)
            total = fdot(active_ref[:count], down_ref[:, at])
            if gated:
                total = total * share
            for place, number in enumerate(members):
                out_refs[number][:, at] = total[place * rows : (place + 1) * rows].astype(BF)


def units(pieces, mark, weights, gated, after):
    parts = len(pieces)
    rows = pieces[0].shape[0]
    hidden, width = weights[2].shape
    group = max(1, min(parts, BLOCK_ROWS // rows))
    outs = pl.pallas_call(
        functools.partial(unit_kernel, gated, parts, group),
        out_shape=[struct(rows, width)] * parts,
        in_specs=[VECTORS] * (4 + parts) + [ANYWHERE] * len(after),
        out_specs=[VECTORS] * parts,
        scratch_shapes=[
            pltpu.VMEM((rows * group, width), BF),
            pltpu.VMEM((rows * group, hidden), BF),
        ],
        compiler_params=SMALL,
        name="experts" if gated else "drafter",
    )(mark, *pieces, *weights, *after)
    return list(outs)


def mid_kernel(count, hid_ref, gain_ref, *refs):
    verified_ref, draft_ref = refs[-2:]
    total = hid_ref[...].astype(F32) + sum(ref[...].astype(F32) for ref in refs[:count])
    verified = total.astype(BF)
    verified_ref[...] = verified
    draft_ref[...] = (rms(verified.astype(F32)) * gain_ref[...]).astype(BF)


def mid(hid, parts, gain, after):
    return pl.pallas_call(
        functools.partial(mid_kernel, len(parts)),
        out_shape=[struct(*hid.shape)] * 2,
        in_specs=[VECTORS] * (2 + len(parts)) + [ANYWHERE] * len(after),
        out_specs=[VECTORS] * 2,
        compiler_params=SMALL,
        name="accepted_norm",
    )(hid, gain, *parts, *after)


def last_kernel(hid_ref, gain_ref, *refs):
    out_ref = refs[-1]
    total = hid_ref[...].astype(F32) + sum(ref[...].astype(F32) for ref in refs[:-1])
    result = (rms(total) * gain_ref[...]).astype(BF).astype(F32)
    requests, rounds, _ = out_ref.shape
    for request in range(requests):
        out_ref[request] = result[request * rounds : (request + 1) * rounds].astype(BF)


def last(hid, parts, gain, requests, rounds):
    return pl.pallas_call(
        last_kernel,
        out_shape=jax.ShapeDtypeStruct((requests, rounds, hid.shape[1]), BF),
        compiler_params=SMALL,
        name="draft_norm",
    )(hid, gain, *parts)


def merge_kernel(groups, accepted_ref, *refs):
    out_ref = refs[-1]
    rows, rounds, _ = out_ref.shape
    requests = accepted_ref.shape[0]
    draft = rows // requests
    chunk = rounds * requests
    layers = []
    first = 0
    for group in groups:
        members = refs[first : first + group]
        first += group
        total = sum(ref[...].astype(F32) for ref in members).astype(BF).astype(F32)
        layers += [total[at : at + chunk] for at in range(0, total.shape[0], chunk)]
    for request in range(requests):
        taken = accepted_vector(accepted_ref, request, rounds)
        held = [layer[request * rounds : (request + 1) * rounds] for layer in layers]
        for inside in range(draft):
            found = held[0]
            if inside < draft - 1:
                found = jnp.where(taken > inside, held[inside + 1], found)
            if inside > 0:
                found = jnp.where(taken < inside, held[inside], found)
            out_ref[request * draft + inside] = found.astype(BF)


def merge(accepted, groups, rows, rounds):
    flat = [array for group in groups for array in group]
    return pl.pallas_call(
        functools.partial(merge_kernel, [len(group) for group in groups]),
        out_shape=jax.ShapeDtypeStruct((rows, rounds, flat[0].shape[1]), BF),
        in_specs=[SCALARS] + [VECTORS] * len(flat),
        out_specs=VECTORS,
        compiler_params=SMALL,
        name="merge",
    )(accepted, *flat)


class Links:

    def __init__(self, lines, columns):
        self.lines = lines
        self.columns = columns

    def line(self, x, bits):
        return lax.ppermute(x, "expert", [(i, i ^ bits) for i in range(self.lines)])

    def far(self, x):
        return lax.ppermute(x, "tensor", [(i, i ^ 2) for i in range(self.columns)])

    def near(self, x):
        return lax.ppermute(x, "tensor", [(i, i ^ 1) for i in range(self.columns)])

    def widen(self, x, bit, after):
        return pack([x, self.line(x, bit)], after)

    def sides(self, x, after):
        own = pack([x, self.far(x)], after, CUT)
        return own + [self.near(piece) for piece in own]

    def meet(self, pieces):
        comes = [self.near(piece) for piece in pieces[CUT:]]
        return [fold(keep, [come], 1, [])[0] for keep, come in zip(pieces, comes)]


def bits_of(size):
    return [1 << bit for bit in reversed(range(size.bit_length() - 1))]


def local(
    lines,
    columns,
    subs,
    hidden_rows,
    expert_ids,
    accepted,
    norm_gain,
    router,
    gate_weight,
    up_weight,
    down_weight,
    draft_gain,
    draft_gate,
    draft_up,
    draft_down,
    final_gain,
):
    rounds, rows, width = hidden_rows.shape
    requests = accepted.shape[1]
    draft = rows // requests
    links = Links(lines, columns)
    accepted = accepted.T
    inputs = (
        accepted,
        hidden_rows.transpose(1, 0, 2),
        expert_ids.transpose(0, 2, 1),
        norm_gain.reshape(1, width),
        router.T,
    )

    def over_sub(terms):
        if subs > 1:
            terms = [lax.psum(sum(term.astype(F32) for term in terms), "sub")]
        return terms

    weights = [gate_weight[0], up_weight[0], down_weight[0]]
    draft_weights = [draft_gate, draft_up, draft_down]
    bits = bits_of(lines)
    chunk = rounds * requests
    others = rounds * rows - chunk
    ext, hid, mark = prep(inputs, [list(range(draft))], columns)
    hid, rest_hid = hid[:chunk], hid[chunk:]

    lined, offsets = [ext], [0]
    for bit in bits:
        lined = lined + [links.line(block, bit) for block in lined]
        offsets = offsets + [offset | bit for offset in offsets]
    crossed = [links.far(block) for block in lined]
    head = [cut(lined, 0, chunk, [], weights[:1]), cut(crossed, 0, chunk, [], weights[1:])]
    head += [links.near(piece) for piece in head]
    line_rest = cut(lined, chunk, others, head[2:])
    cross_rest = cut(crossed, chunk, others, head[2:])
    cross_other = links.near(cross_rest)
    line_other = links.near(line_rest)

    halves = links.meet(units(head, mark, weights, True, []))
    cross_keep, cross_send = units([cross_rest, cross_other], mark, weights, True, [halves[1]])
    steps = []
    keep, come = halves[0], links.far(halves[1])
    for place, bit in enumerate(reversed(bits)):
        waits = [cross_keep] if place == 0 else [line_keep] if place == 1 else []
        keep, send = fold(keep, [come], 2, waits)
        come = links.line(send, bit)
        steps.append(send)
        if place == 0:
            line_keep, line_send = units(
                [line_rest, line_other], mark, weights, True, [send]
            )
    cross_come = links.near(hold([cross_send], [steps[0]])[0])
    line_come = links.near(hold([line_send], [steps[1]])[0])
    features, draft_in = mid(
        hid, over_sub([keep, come]), draft_gain.reshape(1, width), []
    )
    cross_parts = fold(cross_keep, [cross_come], lines, [])
    line_parts = fold(line_keep, [line_come], lines, [])

    held = {}
    for place in reversed(range(lines)):
        held[offsets[place]] = [line_parts[place], links.far(cross_parts[place])]
    summed = {}
    for bit in reversed(bits):
        for offset in reversed(offsets):
            if offset & bit and offset < 2 * bit * (lines // bit) and not offset & (bit - 1):
                summed[offset] = add(held[offset])
                held[offset ^ bit].append(links.line(summed[offset], bit))
    rest_terms = held[0]
    a = draft_in
    for place, bit in enumerate(bits):
        a = links.widen(a, bit, (([cross_parts[0]], [summed[lines - 1], held[lines // 2][1]])[place] if place < 2 else []))
    own = pack([a, links.far(a)], [summed[lines // 2], summed[1]], CUT)
    pieces = own + [links.near(piece) for piece in own]
    halves = links.meet(units(pieces, mark, draft_weights, False, []))
    keep, come = halves[0], links.far(halves[1])
    for bit in reversed(bits):
        keep, send = fold(keep, [come], 2, [])
        come = links.line(send, bit)
    terms = [keep, come]
    draft_out = last(features, terms, final_gain.reshape(1, width), requests, rounds)
    verified = merge(
        accepted,
        [[features], [rest_hid] + over_sub(rest_terms)],
        rows,
        rounds,
    )
    return verified.transpose(1, 0, 2), draft_out.transpose(1, 0, 2)


def solution(mesh):
    placed = (
        P(None, ("groups", "expert", "tensor"), None),
        P(None, ("groups", "expert", "tensor"), None),
        P(None, ("groups", "expert", "tensor")),
        P(),
        P(),
        P(("expert", "tensor"), None, "sub"),
        P(("expert", "tensor"), None, "sub"),
        P(("expert", "tensor"), "sub", None),
        P(),
        P(None, ("expert", "tensor")),
        P(None, ("expert", "tensor")),
        P(("expert", "tensor"), None),
        P(),
    )
    body = functools.partial(
        local, mesh.shape["expert"], mesh.shape["tensor"], mesh.shape["sub"]
    )
    return jax.shard_map(
        body,
        mesh=mesh,
        in_specs=placed,
        out_specs=(
            P(None, ("groups", "expert", "tensor"), None),
            P(None, ("groups", "expert", "tensor"), None),
        ),
        check_vma=False,
    )
```

```python
import functools

import jax
import jax.numpy as jnp
from jax import lax
from jax.experimental import pallas as pl
from jax.experimental.pallas import tpu as pltpu
from jax.sharding import PartitionSpec as P

EPSILON = 1e-06
BF = jnp.bfloat16
F32 = jnp.float32
LANES = 128
MIB = 1024 * 1024
SMALL = pltpu.CompilerParams(vmem_limit_bytes=16 * MIB)
BLOCK_ROWS = 256
CUT = 2
ANYWHERE = pl.BlockSpec(memory_space=pl.ANY)
HBM = pl.BlockSpec(memory_space=pltpu.HBM)
SCALARS = pl.BlockSpec(memory_space=pltpu.SMEM)
VECTORS = pl.BlockSpec(memory_space=pltpu.VMEM)


def fdot(a, b):
    return jnp.dot(a, b, preferred_element_type=F32)


def fdot_t(a, b):
    return lax.dot_general(a, b, (((1,), (1,)), ((), ())), preferred_element_type=F32)


def iota(shape, axis):
    return lax.broadcasted_iota(jnp.int32, shape, axis)


def rms(values):
    return values * lax.rsqrt(jnp.mean(values * values, axis=-1, keepdims=True) + EPSILON)


def struct(rows, columns):
    return jax.ShapeDtypeStruct((rows, columns), BF)


def accepted_vector(accepted_ref, request, rounds):
    place = iota((rounds, 1), 0)
    found = jnp.zeros((rounds, 1), jnp.int32)
    for number in range(rounds):
        found = jnp.where(place == number, accepted_ref[request, number], found)
    return found


def reorder(layers, accepted_ref, hidden_ref, ids_ref, gain_ref, router_ref, ext_ref, hid_ref):
    rows, rounds, width = hidden_ref.shape
    requests = accepted_ref.shape[0]
    draft = rows // requests
    top, experts = ids_ref.shape[1], router_ref.shape[0]
    chunk = rounds * requests
    taken = [accepted_vector(accepted_ref, request, rounds) for request in range(requests)]
    pieces = []
    for layer in layers:
        for request in range(requests):
            first = request * draft
            if layer == 0:
                found = hidden_ref[first].astype(F32)
                for inside in range(1, draft):
                    found = jnp.where(
                        taken[request] == inside, hidden_ref[first + inside].astype(F32), found
                    )
            else:
                found = jnp.where(
                    taken[request] >= layer,
                    hidden_ref[first + layer - 1].astype(F32),
                    hidden_ref[first + layer].astype(F32),
                )
            pieces.append(found)
    raw = jnp.concatenate(pieces, axis=0)
    hid_ref[...] = raw.astype(BF)
    normed = (rms(raw) * gain_ref[...]).astype(BF)
    ext_ref[:, :width] = normed
    count = len(layers) * chunk
    logits = fdot_t(normed, router_ref[...])
    place = iota((count, rows), 0)
    source = iota((count, rows), 1)
    wanted = jnp.full((count, rows), -1, jnp.int32)
    for number, layer in enumerate(layers):
        for request in range(requests):
            for turn in range(rounds):
                value = accepted_ref[request, turn]
                if layer > 0:
                    value = jnp.where(value >= layer, layer - 1, layer)
                row = number * chunk + request * rounds + turn
                wanted = jnp.where(place == row, value + request * draft, wanted)
    chosen = wanted == source
    named = None
    for turn in range(rounds):
        ids = ids_ref[turn]
        expert = iota((experts, rows), 0)
        hot = ids[0:1] == expert
        for k in range(1, top):
            hot = hot | (ids[k : k + 1] == expert)
        pick = (chosen & (lax.rem(place, rounds) == turn)).astype(F32).astype(BF)
        term = fdot_t(pick, hot.astype(F32).astype(BF))
        named = term if named is None else named + term
    powers = jnp.where(named > 0.5, jnp.exp(logits), 0.0)
    share = powers / jnp.sum(powers, axis=1, keepdims=True)
    high = share.astype(BF).astype(F32)
    tail = [high, share - high]
    if 2 * experts < LANES:
        tail.append(jnp.zeros((count, LANES - 2 * experts), F32))
    ext_ref[:, width:] = jnp.concatenate(tail, axis=1).astype(BF)


def prep_kernel(groups, columns, experts, *refs):
    sources, outs, targets, sems = refs[:5], refs[5:-6], refs[-6:-1], refs[-1]
    moves = [
        pltpu.make_async_copy(source, target, sems.at[number])
        for number, (source, target) in enumerate(zip(sources, targets))
    ]
    for move in moves:
        move.start()
    me = lax.axis_index("expert") * columns + lax.axis_index("tensor")
    lane = iota((1, LANES), 1)
    outs[-1][...] = ((lane == me) | (lane == me + experts)).astype(F32)
    for move in moves:
        move.wait()
    for number, layers in enumerate(groups):
        reorder(layers, *targets, outs[2 * number], outs[2 * number + 1])


def prep(inputs, groups, columns):
    accepted, hidden = inputs[:2]
    rows, rounds, width = hidden.shape
    shapes = []
    for layers in groups:
        count = len(layers) * rounds * accepted.shape[0]
        shapes += [struct(count, width + LANES), struct(count, width)]
    shapes.append(jax.ShapeDtypeStruct((1, LANES), F32))
    return pl.pallas_call(
        functools.partial(prep_kernel, groups, columns, inputs[-1].shape[0]),
        out_shape=shapes,
        in_specs=[HBM] * 5,
        out_specs=[VECTORS] * len(shapes),
        scratch_shapes=[pltpu.SMEM(accepted.shape, jnp.int32)]
        + [pltpu.VMEM(array.shape, array.dtype) for array in inputs[1:]]
        + [pltpu.SemaphoreType.DMA((5,))],
        compiler_params=pltpu.CompilerParams(vmem_limit_bytes=56 * MIB),
        name="prep",
    )(*inputs)


def hold(arrays, after):
    held = pl.pallas_call(
        lambda *refs: None,
        out_shape=[struct(*array.shape) for array in arrays],
        in_specs=[ANYWHERE] * (len(arrays) + len(after)),
        out_specs=[ANYWHERE] * len(arrays),
        input_output_aliases={number: number for number in range(len(arrays))},
        compiler_params=SMALL,
        name="hold",
    )(*arrays, *after)
    return list(held)


def pack_kernel(count, cut, *refs):
    whole = jnp.concatenate([ref[...] for ref in refs[:count]], axis=0)
    rows = whole.shape[0] // cut
    for number, out_ref in enumerate(refs[-cut:]):
        out_ref[...] = whole[number * rows : (number + 1) * rows]


def pack(blocks, after, cut=1):
    rows, width = sum(block.shape[0] for block in blocks), blocks[0].shape[1]
    outs = pl.pallas_call(
        functools.partial(pack_kernel, len(blocks), cut),
        out_shape=[struct(rows // cut, width)] * cut,
        in_specs=[VECTORS] * len(blocks) + [ANYWHERE] * len(after),
        out_specs=[VECTORS] * cut,
        compiler_params=SMALL,
        name="pack",
    )(*blocks, *after)
    return outs[0] if cut == 1 else list(outs)


def cut_kernel(count, first, rows, *refs):
    blocks = [ref[...] for ref in refs[:count]]
    refs[-1][...] = jnp.concatenate([block[first : first + rows] for block in blocks], axis=0)


def cut(blocks, first, rows, after, near=()):
    width = blocks[0].shape[1]
    count = len(blocks)
    return pl.pallas_call(
        functools.partial(cut_kernel, count, first, rows),
        out_shape=struct(count * rows, width),
        in_specs=[VECTORS] * count + [ANYWHERE] * len(after) + [VECTORS] * len(near),
        out_specs=VECTORS,
        compiler_params=SMALL,
        name="cut",
    )(*blocks, *after, *near)


def stage_kernel(count, *refs):
    sources, targets, sems = refs[:count], refs[-count - 1 : -1], refs[-1]
    moves = [
        pltpu.make_async_copy(source, target, sems.at[number])
        for number, (source, target) in enumerate(zip(sources, targets))
    ]
    for move in moves:
        move.start()
    for move in moves:
        move.wait()


def stage(arrays, limit, after):
    count = len(arrays)
    outs = pl.pallas_call(
        functools.partial(stage_kernel, count),
        out_shape=[struct(*array.shape) for array in arrays],
        in_specs=[HBM] * count + [ANYWHERE] * len(after),
        out_specs=[VECTORS] * count,
        scratch_shapes=[pltpu.SemaphoreType.DMA((count,))],
        compiler_params=pltpu.CompilerParams(vmem_limit_bytes=limit * MIB),
        name="stage",
    )(*arrays, *after)
    return list(outs)


def add_kernel(count, parts, *refs):
    total = sum(ref[...].astype(F32) for ref in refs[:count]).astype(BF)
    rows = total.shape[0] // parts
    for number, out_ref in enumerate(refs[-parts:]):
        out_ref[...] = total[number * rows : (number + 1) * rows]


def add(arrays, after=(), parts=1):
    rows, width = arrays[0].shape
    outs = pl.pallas_call(
        functools.partial(add_kernel, len(arrays), parts),
        out_shape=[struct(rows // parts, width)] * parts,
        in_specs=[VECTORS] * len(arrays) + [ANYWHERE] * len(after),
        out_specs=[VECTORS] * parts,
        compiler_params=SMALL,
        name="add",
    )(*arrays, *after)
    return outs[0] if parts == 1 else list(outs)


def fold_kernel(comes, parts, keep_ref, *refs):
    come_refs, out_refs = refs[:comes], refs[-parts:]
    rows = out_refs[0].shape[0]
    come = jnp.concatenate([ref[...] for ref in come_refs], axis=0).astype(F32)
    total = keep_ref[...].astype(F32) + come
    for number, out_ref in enumerate(out_refs):
        out_ref[...] = total[number * rows : (number + 1) * rows].astype(BF)


def fold(keep, comes, parts, after):
    rows, width = keep.shape
    return pl.pallas_call(
        functools.partial(fold_kernel, len(comes), parts),
        out_shape=[struct(rows // parts, width)] * parts,
        in_specs=[VECTORS] * (1 + len(comes)) + [ANYWHERE] * len(after),
        out_specs=[VECTORS] * parts,
        compiler_params=SMALL,
        name="fold",
    )(keep, *comes, *after)


def unit_kernel(gated, parts, group, mark_ref, *refs):
    x_refs, (gate_ref, up_ref, down_ref) = refs[:parts], refs[parts : parts + 3]
    out_refs, (all_ref, active_ref) = refs[-parts - 2 : -2], refs[-2:]
    rows, width = out_refs[0].shape
    hidden = gate_ref.shape[1]
    tile = min(256, hidden)
    columns = min(512, width)
    for first in range(0, parts, group):
        members = list(range(first, min(first + group, parts)))
        count = len(members) * rows
        for place, number in enumerate(members):
            all_ref[place * rows : (place + 1) * rows] = x_refs[number][:, :width]

        for step in range(0, hidden, tile):
            at = slice(step, step + tile)
            gate = fdot(all_ref[:count], gate_ref[:, at])
            up = fdot(all_ref[:count], up_ref[:, at])
            active_ref[:count, at] = (gate / (1.0 + jnp.exp(-gate)) * up).astype(BF)

        share = None
        if gated:
            tail = jnp.concatenate([x_refs[number][:, width:] for number in members], axis=0)
            share = jnp.sum(tail.astype(F32) * mark_ref[...], axis=1, keepdims=True)

        for step in range(0, width, columns):
            at = slice(step, step + columns)
            total = fdot(active_ref[:count], down_ref[:, at])
            if gated:
                total = total * share
            for place, number in enumerate(members):
                out_refs[number][:, at] = total[place * rows : (place + 1) * rows].astype(BF)


def units(pieces, mark, weights, gated, after):
    parts = len(pieces)
    rows = pieces[0].shape[0]
    hidden, width = weights[2].shape
    group = max(1, min(parts, BLOCK_ROWS // rows))
    outs = pl.pallas_call(
        functools.partial(unit_kernel, gated, parts, group),
        out_shape=[struct(rows, width)] * parts,
        in_specs=[VECTORS] * (4 + parts) + [ANYWHERE] * len(after),
        out_specs=[VECTORS] * parts,
        scratch_shapes=[
            pltpu.VMEM((rows * group, width), BF),
            pltpu.VMEM((rows * group, hidden), BF),
        ],
        compiler_params=SMALL,
        name="experts" if gated else "drafter",
    )(mark, *pieces, *weights, *after)
    return list(outs)


def mid_kernel(swapped, hid_ref, other_ref, gain_ref, held_ref, *refs):
    verified_ref, draft_ref = refs[-2:]
    rows = hid_ref.shape[0]
    held = held_ref[...].astype(F32)
    own, other = held[:rows], held[rows:]
    if swapped:
        come = refs[0][...].astype(F32)
        own, other = own + come[rows:], other + come[:rows]
    verified = (hid_ref[...].astype(F32) + own).astype(BF)
    verified_ref[...] = verified
    beside = (other_ref[...].astype(F32) + other).astype(BF)
    both = jnp.concatenate([verified.astype(F32), beside.astype(F32)], axis=0)
    draft_ref[...] = (rms(both) * gain_ref[...]).astype(BF)


def mid(hid, other, sums, gain, after):
    return pl.pallas_call(
        functools.partial(mid_kernel, len(sums) > 1),
        out_shape=[struct(*hid.shape), struct(2 * hid.shape[0], hid.shape[1])],
        in_specs=[VECTORS] * (3 + len(sums)) + [ANYWHERE] * len(after),
        out_specs=[VECTORS] * 2,
        compiler_params=SMALL,
        name="accepted_norm",
    )(hid, other, gain, *sums, *after)


def last_kernel(hid_ref, gain_ref, *refs):
    out_ref = refs[-1]
    total = hid_ref[...].astype(F32) + sum(ref[...].astype(F32) for ref in refs[:-1])
    result = (rms(total) * gain_ref[...]).astype(BF).astype(F32)
    requests, rounds, _ = out_ref.shape
    for request in range(requests):
        out_ref[request] = result[request * rounds : (request + 1) * rounds].astype(BF)


def last(hid, parts, gain, requests, rounds):
    return pl.pallas_call(
        last_kernel,
        out_shape=jax.ShapeDtypeStruct((requests, rounds, hid.shape[1]), BF),
        compiler_params=SMALL,
        name="draft_norm",
    )(hid, gain, *parts)


def merge_kernel(groups, accepted_ref, *refs):
    out_ref = refs[-1]
    rows, rounds, _ = out_ref.shape
    requests = accepted_ref.shape[0]
    draft = rows // requests
    chunk = rounds * requests
    layers = []
    first = 0
    for group in groups:
        members = refs[first : first + group]
        first += group
        total = sum(ref[...].astype(F32) for ref in members).astype(BF).astype(F32)
        layers += [total[at : at + chunk] for at in range(0, total.shape[0], chunk)]
    for request in range(requests):
        taken = accepted_vector(accepted_ref, request, rounds)
        held = [layer[request * rounds : (request + 1) * rounds] for layer in layers]
        for inside in range(draft):
            found = held[0]
            if inside < draft - 1:
                found = jnp.where(taken > inside, held[inside + 1], found)
            if inside > 0:
                found = jnp.where(taken < inside, held[inside], found)
            out_ref[request * draft + inside] = found.astype(BF)


def merge(accepted, groups, rows, rounds):
    flat = [array for group in groups for array in group]
    return pl.pallas_call(
        functools.partial(merge_kernel, [len(group) for group in groups]),
        out_shape=jax.ShapeDtypeStruct((rows, rounds, flat[0].shape[1]), BF),
        in_specs=[SCALARS] + [VECTORS] * len(flat),
        out_specs=VECTORS,
        compiler_params=SMALL,
        name="merge",
    )(accepted, *flat)


class Links:

    def __init__(self, lines, columns):
        self.lines = lines
        self.columns = columns

    def line(self, x, bits):
        return lax.ppermute(x, "expert", [(i, i ^ bits) for i in range(self.lines)])

    def far(self, x):
        return lax.ppermute(x, "tensor", [(i, i ^ 2) for i in range(self.columns)])

    def near(self, x):
        return lax.ppermute(x, "tensor", [(i, i ^ 1) for i in range(self.columns)])

    def meet(self, pieces):
        comes = [self.near(piece) for piece in pieces[2:]]
        return [fold(keep, [come], 2, []) for keep, come in zip(pieces, comes)]

    def meet_line(self, halves, first_waits, second_waits):
        (keep_even, keep_odd), (send_even, send_odd) = halves
        bits = bits_of(self.lines)
        odd = add([keep_odd, self.far(send_odd)], first_waits)
        come_even = self.far(send_even)
        parts = 1 if len(bits) < 3 else 2
        held = add([keep_even, come_even, self.line(odd, bits[-1])], second_waits(odd), parts)
        for place, bit in enumerate(reversed(bits[1:-1])):
            keep, send = held
            held = add([keep, self.line(send, bit)], [], 1 if place == len(bits) - 3 else 2)
        return held


def bits_of(size):
    return [1 << bit for bit in reversed(range(size.bit_length() - 1))]


def local(
    lines,
    columns,
    subs,
    hidden_rows,
    expert_ids,
    accepted,
    norm_gain,
    router,
    gate_weight,
    up_weight,
    down_weight,
    draft_gain,
    draft_gate,
    draft_up,
    draft_down,
    final_gain,
):
    rounds, rows, width = hidden_rows.shape
    requests = accepted.shape[1]
    draft = rows // requests
    links = Links(lines, columns)
    accepted = accepted.T
    inputs = (
        accepted,
        hidden_rows.transpose(1, 0, 2),
        expert_ids.transpose(0, 2, 1),
        norm_gain.reshape(1, width),
        router.T,
    )

    def over_sub(terms):
        if subs > 1:
            terms = [lax.psum(sum(term.astype(F32) for term in terms), "sub")]
        return terms

    weights = [gate_weight[0], up_weight[0], down_weight[0]]
    draft_weights = [draft_gate, draft_up, draft_down]
    bits = bits_of(lines)
    chunk = rounds * requests
    others = rounds * rows - chunk
    ext, hid, mark = prep(inputs, [list(range(draft))], columns)
    hid, rest_hid = hid[:chunk], hid[chunk:]
    hid_beside = links.line(hid, bits[0])

    lined, offsets, crossed = [ext], [0], [links.far(ext)]
    for bit in bits:
        came = [links.line(block, bit) for block in lined]
        if bit == bits[0]:
            came = hold(came, crossed[-1:])
        lined = lined + came
        offsets = offsets + [offset | bit for offset in offsets]
        crossed = crossed + [links.far(block) for block in came]
    weights = stage(weights, 36, [lined[-1]])
    head = [cut(lined, 0, chunk, [weights[0]], []), cut(crossed, 0, chunk, [hid_beside])]
    head += [links.near(piece) for piece in head]
    line_rest = cut(lined, chunk, others, head[2:])
    cross_rest = cut(crossed, chunk, others, head[2:])
    cross_other = links.near(cross_rest)
    line_other = links.near(line_rest)

    halves = links.meet(units(head, mark, weights, True, []))
    cross_keep, cross_send = units([cross_rest, cross_other], mark, weights, True, [halves[1][1]])
    lines_done = []

    def second_waits(odd):
        cross_come = links.near(hold([cross_send], [odd])[0])
        parts = fold(cross_keep, [cross_come], lines, [])
        lines_done.extend([odd, parts])
        lines_done.extend(units([line_rest, line_other], mark, weights, True, [odd]))
        return [lines_done[2]]

    held = links.meet_line(halves, [cross_keep], second_waits)
    odd, cross_parts, line_keep, line_send = lines_done
    come = links.line(held, bits[0])
    line_come = links.near(hold([line_send], [held])[0])
    sums = [held, come]
    if subs > 1:
        come = jnp.concatenate([come[chunk:], come[:chunk]], axis=0)
        sums = [lax.psum(held.astype(F32) + come.astype(F32), "sub")]
    line_parts = fold(line_keep, [line_come], lines, [])

    blocks = {}
    for place in reversed(range(lines)):
        blocks[offsets[place]] = [line_parts[place], links.far(cross_parts[place])]
    summed = {}
    for bit in reversed(bits):
        for offset in reversed(offsets):
            if offset & bit and offset < 2 * bit * (lines // bit) and not offset & (bit - 1):
                summed[offset] = add(blocks[offset])
                blocks[offset ^ bit].append(links.line(summed[offset], bit))
    rest_terms = blocks[0]
    features, draft_in = mid(hid, hid_beside, sums, draft_gain.reshape(1, width), [summed[lines - 1], blocks[lines // 2][1]])
    a_lined = [draft_in]
    for bit in bits[1:]:
        a_lined = a_lined + [links.line(block, bit) for block in a_lined]
    a_crossed = [links.far(block) for block in a_lined]
    own = [pack(a_lined, [summed[1]]), pack(a_crossed, [])]
    pieces = own + [links.near(piece) for piece in own]
    halves = links.meet(units(pieces, mark, draft_weights, False, [summed[lines // 2]]))
    held = links.meet_line(halves, [], lambda odd: [])
    keep, send = add([held], [], 2)
    terms = [keep, links.line(send, bits[0])]

    draft_out = last(features, terms, final_gain.reshape(1, width), requests, rounds)
    verified = merge(
        accepted,
        [[features], [rest_hid] + over_sub(rest_terms)],
        rows,
        rounds,
    )
    return verified.transpose(1, 0, 2), draft_out.transpose(1, 0, 2)


def solution(mesh):
    placed = (
        P(None, ("groups", "expert", "tensor"), None),
        P(None, ("groups", "expert", "tensor"), None),
        P(None, ("groups", "expert", "tensor")),
        P(),
        P(),
        P(("expert", "tensor"), None, "sub"),
        P(("expert", "tensor"), None, "sub"),
        P(("expert", "tensor"), "sub", None),
        P(),
        P(None, ("expert", "tensor")),
        P(None, ("expert", "tensor")),
        P(("expert", "tensor"), None),
        P(),
    )
    body = functools.partial(
        local, mesh.shape["expert"], mesh.shape["tensor"], mesh.shape["sub"]
    )
    return jax.shard_map(
        body,
        mesh=mesh,
        in_specs=placed,
        out_specs=(
            P(None, ("groups", "expert", "tensor"), None),
            P(None, ("groups", "expert", "tensor"), None),
        ),
        check_vma=False,
    )
```

```python
import functools

import jax
import jax.numpy as jnp
from jax import lax
from jax.experimental import pallas as pl
from jax.experimental.pallas import tpu as pltpu
from jax.sharding import PartitionSpec as P

EPSILON = 1e-06
BF = jnp.bfloat16
F32 = jnp.float32
LANES = 128
MIB = 1024 * 1024
SMALL = pltpu.CompilerParams(vmem_limit_bytes=16 * MIB)
BLOCK_ROWS = 256
CUT = 2
ANYWHERE = pl.BlockSpec(memory_space=pl.ANY)
HBM = pl.BlockSpec(memory_space=pltpu.HBM)
SCALARS = pl.BlockSpec(memory_space=pltpu.SMEM)
VECTORS = pl.BlockSpec(memory_space=pltpu.VMEM)


def fdot(a, b):
    return jnp.dot(a, b, preferred_element_type=F32)


def fdot_t(a, b):
    return lax.dot_general(a, b, (((1,), (1,)), ((), ())), preferred_element_type=F32)


def iota(shape, axis):
    return lax.broadcasted_iota(jnp.int32, shape, axis)


def rms(values):
    return values * lax.rsqrt(jnp.mean(values * values, axis=-1, keepdims=True) + EPSILON)


def struct(rows, columns):
    return jax.ShapeDtypeStruct((rows, columns), BF)


def accepted_vector(accepted_ref, request, rounds):
    place = iota((rounds, 1), 0)
    found = jnp.zeros((rounds, 1), jnp.int32)
    for number in range(rounds):
        found = jnp.where(place == number, accepted_ref[request, number], found)
    return found


def reorder(layers, accepted_ref, hidden_ref, ids_ref, gain_ref, router_ref, ext_ref, hid_ref, more_ref):
    rows, rounds, width = hidden_ref.shape
    requests = accepted_ref.shape[0]
    draft = rows // requests
    top, experts = ids_ref.shape[1], router_ref.shape[0]
    chunk = rounds * requests
    taken = [accepted_vector(accepted_ref, request, rounds) for request in range(requests)]
    pieces = []
    for layer in layers:
        for request in range(requests):
            first = request * draft
            if layer == 0:
                found = hidden_ref[first].astype(F32)
                for inside in range(1, draft):
                    found = jnp.where(
                        taken[request] == inside, hidden_ref[first + inside].astype(F32), found
                    )
            else:
                found = jnp.where(
                    taken[request] >= layer,
                    hidden_ref[first + layer - 1].astype(F32),
                    hidden_ref[first + layer].astype(F32),
                )
            pieces.append(found)
    raw = jnp.concatenate(pieces, axis=0)
    hid_ref[...] = raw[:chunk].astype(BF)
    more_ref[...] = raw[chunk:].astype(BF)
    normed = (rms(raw) * gain_ref[...]).astype(BF)
    ext_ref[:, :width] = normed
    count = len(layers) * chunk
    logits = fdot_t(normed, router_ref[...])
    place = iota((count, rows), 0)
    source = iota((count, rows), 1)
    wanted = jnp.full((count, rows), -1, jnp.int32)
    for number, layer in enumerate(layers):
        for request in range(requests):
            for turn in range(rounds):
                value = accepted_ref[request, turn]
                if layer > 0:
                    value = jnp.where(value >= layer, layer - 1, layer)
                row = number * chunk + request * rounds + turn
                wanted = jnp.where(place == row, value + request * draft, wanted)
    chosen = wanted == source
    named = None
    for turn in range(rounds):
        ids = ids_ref[turn]
        expert = iota((experts, rows), 0)
        hot = ids[0:1] == expert
        for k in range(1, top):
            hot = hot | (ids[k : k + 1] == expert)
        pick = (chosen & (lax.rem(place, rounds) == turn)).astype(F32).astype(BF)
        term = fdot_t(pick, hot.astype(F32).astype(BF))
        named = term if named is None else named + term
    powers = jnp.where(named > 0.5, jnp.exp(logits), 0.0)
    share = powers / jnp.sum(powers, axis=1, keepdims=True)
    high = share.astype(BF).astype(F32)
    tail = [high, share - high]
    if 2 * experts < LANES:
        tail.append(jnp.zeros((count, LANES - 2 * experts), F32))
    ext_ref[:, width:] = jnp.concatenate(tail, axis=1).astype(BF)


def prep_kernel(groups, columns, experts, *refs):
    sources, outs, targets, sems = refs[:5], refs[5:-6], refs[-6:-1], refs[-1]
    moves = [
        pltpu.make_async_copy(source, target, sems.at[number])
        for number, (source, target) in enumerate(zip(sources, targets))
    ]
    for move in moves:
        move.start()
    me = lax.axis_index("expert") * columns + lax.axis_index("tensor")
    lane = iota((1, LANES), 1)
    outs[-1][...] = ((lane == me) | (lane == me + experts)).astype(F32)
    for move in moves:
        move.wait()
    for number, layers in enumerate(groups):
        reorder(layers, *targets, *outs[3 * number : 3 * number + 3])


def prep(inputs, groups, columns):
    accepted, hidden = inputs[:2]
    rows, rounds, width = hidden.shape
    shapes = []
    for layers in groups:
        count = len(layers) * rounds * accepted.shape[0]
        chunk = rounds * accepted.shape[0]
        shapes += [struct(count, width + LANES), struct(chunk, width), struct(count - chunk, width)]
    shapes.append(jax.ShapeDtypeStruct((1, LANES), F32))
    return pl.pallas_call(
        functools.partial(prep_kernel, groups, columns, inputs[-1].shape[0]),
        out_shape=shapes,
        in_specs=[HBM] * 5,
        out_specs=[VECTORS] * len(shapes),
        scratch_shapes=[pltpu.SMEM(accepted.shape, jnp.int32)]
        + [pltpu.VMEM(array.shape, array.dtype) for array in inputs[1:]]
        + [pltpu.SemaphoreType.DMA((5,))],
        compiler_params=pltpu.CompilerParams(vmem_limit_bytes=56 * MIB),
        name="prep",
    )(*inputs)


def hold(arrays, after):
    held = pl.pallas_call(
        lambda *refs: None,
        out_shape=[struct(*array.shape) for array in arrays],
        in_specs=[ANYWHERE] * (len(arrays) + len(after)),
        out_specs=[ANYWHERE] * len(arrays),
        input_output_aliases={number: number for number in range(len(arrays))},
        compiler_params=SMALL,
        name="hold",
    )(*arrays, *after)
    return list(held)


def pack_kernel(count, cut, *refs):
    whole = jnp.concatenate([ref[...] for ref in refs[:count]], axis=0)
    rows = whole.shape[0] // cut
    for number, out_ref in enumerate(refs[-cut:]):
        out_ref[...] = whole[number * rows : (number + 1) * rows]


def pack(blocks, after, cut=1):
    rows, width = sum(block.shape[0] for block in blocks), blocks[0].shape[1]
    outs = pl.pallas_call(
        functools.partial(pack_kernel, len(blocks), cut),
        out_shape=[struct(rows // cut, width)] * cut,
        in_specs=[VECTORS] * len(blocks) + [ANYWHERE] * len(after),
        out_specs=[VECTORS] * cut,
        compiler_params=SMALL,
        name="pack",
    )(*blocks, *after)
    return outs[0] if cut == 1 else list(outs)


def cut_kernel(count, first, rows, *refs):
    blocks = [ref[...] for ref in refs[:count]]
    refs[-1][...] = jnp.concatenate([block[first : first + rows] for block in blocks], axis=0)


def cut(blocks, first, rows, after, near=()):
    width = blocks[0].shape[1]
    count = len(blocks)
    return pl.pallas_call(
        functools.partial(cut_kernel, count, first, rows),
        out_shape=struct(count * rows, width),
        in_specs=[VECTORS] * count + [ANYWHERE] * len(after) + [VECTORS] * len(near),
        out_specs=VECTORS,
        compiler_params=SMALL,
        name="cut",
    )(*blocks, *after, *near)


def stage_kernel(count, *refs):
    sources, targets, sems = refs[:count], refs[-count - 1 : -1], refs[-1]
    moves = [
        pltpu.make_async_copy(source, target, sems.at[number])
        for number, (source, target) in enumerate(zip(sources, targets))
    ]
    for move in moves:
        move.start()
    for move in moves:
        move.wait()


def stage(arrays, limit, after):
    count = len(arrays)
    outs = pl.pallas_call(
        functools.partial(stage_kernel, count),
        out_shape=[struct(*array.shape) for array in arrays],
        in_specs=[HBM] * count + [ANYWHERE] * len(after),
        out_specs=[VECTORS] * count,
        scratch_shapes=[pltpu.SemaphoreType.DMA((count,))],
        compiler_params=pltpu.CompilerParams(vmem_limit_bytes=limit * MIB),
        name="stage",
    )(*arrays, *after)
    return list(outs)


def add_kernel(count, parts, *refs):
    total = sum(ref[...].astype(F32) for ref in refs[:count]).astype(BF)
    rows = total.shape[0] // parts
    for number, out_ref in enumerate(refs[-parts:]):
        out_ref[...] = total[number * rows : (number + 1) * rows]


def add(arrays, after=(), parts=1):
    rows, width = arrays[0].shape
    outs = pl.pallas_call(
        functools.partial(add_kernel, len(arrays), parts),
        out_shape=[struct(rows // parts, width)] * parts,
        in_specs=[VECTORS] * len(arrays) + [ANYWHERE] * len(after),
        out_specs=[VECTORS] * parts,
        compiler_params=SMALL,
        name="add",
    )(*arrays, *after)
    return outs[0] if parts == 1 else list(outs)


def fold_kernel(comes, parts, keep_ref, *refs):
    come_refs, out_refs = refs[:comes], refs[-parts:]
    rows = out_refs[0].shape[0]
    come = jnp.concatenate([ref[...] for ref in come_refs], axis=0).astype(F32)
    total = keep_ref[...].astype(F32) + come
    for number, out_ref in enumerate(out_refs):
        out_ref[...] = total[number * rows : (number + 1) * rows].astype(BF)


def fold(keep, comes, parts, after):
    rows, width = keep.shape
    return pl.pallas_call(
        functools.partial(fold_kernel, len(comes), parts),
        out_shape=[struct(rows // parts, width)] * parts,
        in_specs=[VECTORS] * (1 + len(comes)) + [ANYWHERE] * len(after),
        out_specs=[VECTORS] * parts,
        compiler_params=SMALL,
        name="fold",
    )(keep, *comes, *after)


def unit_kernel(gated, parts, group, mark_ref, *refs):
    x_refs, (gate_ref, up_ref, down_ref) = refs[:parts], refs[parts : parts + 3]
    out_refs, (all_ref, active_ref) = refs[-parts - 2 : -2], refs[-2:]
    rows, width = out_refs[0].shape
    hidden = gate_ref.shape[1]
    tile = min(256, hidden)
    columns = min(512, width)
    for first in range(0, parts, group):
        members = list(range(first, min(first + group, parts)))
        count = len(members) * rows
        for place, number in enumerate(members):
            all_ref[place * rows : (place + 1) * rows] = x_refs[number][:, :width]

        for step in range(0, hidden, tile):
            at = slice(step, step + tile)
            gate = fdot(all_ref[:count], gate_ref[:, at])
            up = fdot(all_ref[:count], up_ref[:, at])
            active_ref[:count, at] = (gate / (1.0 + jnp.exp(-gate)) * up).astype(BF)

        share = None
        if gated:
            tail = jnp.concatenate([x_refs[number][:, width:] for number in members], axis=0)
            share = jnp.sum(tail.astype(F32) * mark_ref[...], axis=1, keepdims=True)

        for step in range(0, width, columns):
            at = slice(step, step + columns)
            total = fdot(active_ref[:count], down_ref[:, at])
            if gated:
                total = total * share
            for place, number in enumerate(members):
                out_refs[number][:, at] = total[place * rows : (place + 1) * rows].astype(BF)


def units(pieces, mark, weights, gated, after):
    parts = len(pieces)
    rows = pieces[0].shape[0]
    hidden, width = weights[2].shape
    group = max(1, min(parts, BLOCK_ROWS // rows))
    outs = pl.pallas_call(
        functools.partial(unit_kernel, gated, parts, group),
        out_shape=[struct(rows, width)] * parts,
        in_specs=[VECTORS] * (4 + parts) + [ANYWHERE] * len(after),
        out_specs=[VECTORS] * parts,
        scratch_shapes=[
            pltpu.VMEM((rows * group, width), BF),
            pltpu.VMEM((rows * group, hidden), BF),
        ],
        compiler_params=SMALL,
        name="experts" if gated else "drafter",
    )(mark, *pieces, *weights, *after)
    return list(outs)


def mid_kernel(swapped, hid_ref, other_ref, gain_ref, held_ref, *refs):
    verified_ref, draft_ref = refs[-2:]
    rows = hid_ref.shape[0]
    held = held_ref[...].astype(F32)
    own, other = held[:rows], held[rows:]
    if swapped:
        come = refs[0][...].astype(F32)
        own, other = own + come[rows:], other + come[:rows]
    verified = (hid_ref[...].astype(F32) + own).astype(BF)
    verified_ref[...] = verified
    beside = (other_ref[...].astype(F32) + other).astype(BF)
    both = jnp.concatenate([verified.astype(F32), beside.astype(F32)], axis=0)
    draft_ref[...] = (rms(both) * gain_ref[...]).astype(BF)


def mid(hid, other, sums, gain, after):
    return pl.pallas_call(
        functools.partial(mid_kernel, len(sums) > 1),
        out_shape=[struct(*hid.shape), struct(2 * hid.shape[0], hid.shape[1])],
        in_specs=[VECTORS] * (3 + len(sums)) + [ANYWHERE] * len(after),
        out_specs=[VECTORS] * 2,
        compiler_params=SMALL,
        name="accepted_norm",
    )(hid, other, gain, *sums, *after)


def last_kernel(hid_ref, gain_ref, *refs):
    out_ref = refs[-1]
    total = hid_ref[...].astype(F32) + sum(ref[...].astype(F32) for ref in refs[:-1])
    result = (rms(total) * gain_ref[...]).astype(BF).astype(F32)
    rounds, requests, _ = out_ref.shape
    for turn in range(rounds):
        members = [result[turn + request * rounds][None] for request in range(requests)]
        out_ref[turn] = jnp.concatenate(members, axis=0).astype(BF)


def last(hid, parts, gain, requests, rounds):
    return pl.pallas_call(
        last_kernel,
        out_shape=jax.ShapeDtypeStruct((rounds, requests, hid.shape[1]), BF),
        compiler_params=SMALL,
        name="draft_norm",
    )(hid, gain, *parts)


def merge_kernel(groups, accepted_ref, *refs):
    out_ref = refs[-1]
    rows, rounds, _ = out_ref.shape
    requests = accepted_ref.shape[0]
    draft = rows // requests
    chunk = rounds * requests
    layers = []
    first = 0
    for group in groups:
        members = refs[first : first + group]
        first += group
        total = sum(ref[...].astype(F32) for ref in members).astype(BF).astype(F32)
        layers += [total[at : at + chunk] for at in range(0, total.shape[0], chunk)]
    for request in range(requests):
        taken = accepted_vector(accepted_ref, request, rounds)
        held = [layer[request * rounds : (request + 1) * rounds] for layer in layers]
        for inside in range(draft):
            found = held[0]
            if inside < draft - 1:
                found = jnp.where(taken > inside, held[inside + 1], found)
            if inside > 0:
                found = jnp.where(taken < inside, held[inside], found)
            out_ref[request * draft + inside] = found.astype(BF)


def merge(accepted, groups, rows, rounds):
    flat = [array for group in groups for array in group]
    return pl.pallas_call(
        functools.partial(merge_kernel, [len(group) for group in groups]),
        out_shape=jax.ShapeDtypeStruct((rows, rounds, flat[0].shape[1]), BF),
        in_specs=[SCALARS] + [VECTORS] * len(flat),
        out_specs=VECTORS,
        compiler_params=SMALL,
        name="merge",
    )(accepted, *flat)


class Links:

    def __init__(self, lines, columns):
        self.lines = lines
        self.columns = columns

    def line(self, x, bits):
        return lax.ppermute(x, "expert", [(i, i ^ bits) for i in range(self.lines)])

    def far(self, x):
        return lax.ppermute(x, "tensor", [(i, i ^ 2) for i in range(self.columns)])

    def near(self, x):
        return lax.ppermute(x, "tensor", [(i, i ^ 1) for i in range(self.columns)])

    def meet(self, pieces):
        comes = [self.near(piece) for piece in pieces[2:]]
        return [fold(keep, [come], 2, []) for keep, come in zip(pieces, comes)]

    def meet_line(self, halves, first_waits, second_waits):
        (keep_even, keep_odd), (send_even, send_odd) = halves
        bits = bits_of(self.lines)
        odd = add([keep_odd, self.far(send_odd)], first_waits)
        come_even = self.far(send_even)
        parts = 1 if len(bits) < 3 else 2
        held = add([keep_even, come_even, self.line(odd, bits[-1])], second_waits(odd), parts)
        for place, bit in enumerate(reversed(bits[1:-1])):
            keep, send = held
            held = add([keep, self.line(send, bit)], [], 1 if place == len(bits) - 3 else 2)
        return held


def bits_of(size):
    return [1 << bit for bit in reversed(range(size.bit_length() - 1))]


def local(
    lines,
    columns,
    subs,
    hidden_rows,
    expert_ids,
    accepted,
    norm_gain,
    router,
    gate_weight,
    up_weight,
    down_weight,
    draft_gain,
    draft_gate,
    draft_up,
    draft_down,
    final_gain,
):
    rounds, rows, width = hidden_rows.shape
    requests = accepted.shape[1]
    draft = rows // requests
    links = Links(lines, columns)
    accepted = accepted.T
    inputs = (
        accepted,
        hidden_rows.transpose(1, 0, 2),
        expert_ids.transpose(0, 2, 1),
        norm_gain.reshape(1, width),
        router.T,
    )

    def over_sub(terms):
        if subs > 1:
            terms = [lax.psum(sum(term.astype(F32) for term in terms), "sub")]
        return terms

    weights = [gate_weight[0], up_weight[0], down_weight[0]]
    draft_weights = [draft_gate, draft_up, draft_down]
    bits = bits_of(lines)
    chunk = rounds * requests
    others = rounds * rows - chunk
    ext, hid, rest_hid, mark = prep(inputs, [list(range(draft))], columns)
    hid_beside = links.line(hid, bits[0])

    lined, offsets, crossed = [ext], [0], [links.far(ext)]
    for bit in bits:
        came = [links.line(block, bit) for block in lined[len(lined) > 1 :]]
        if len(lined) > 1:
            came = [near_line] + came
        if bit == bits[0]:
            near_line = links.line(ext, bits[-1])
            came = hold(came, [crossed[0], near_line])
        lined = lined + came
        offsets = offsets + [offset | bit for offset in offsets]
        crossed = crossed + [links.far(block) for block in came]
    weights = stage(weights, 36, [lined[-1]])
    head = [cut(lined, 0, chunk, [weights[0]], []), cut(crossed, 0, chunk, [hid_beside])]
    head += [links.near(piece) for piece in head]
    line_rest = cut(lined, chunk, others, head[2:])
    cross_rest = cut(crossed, chunk, others, head[2:])
    cross_other = links.near(cross_rest)
    line_other = links.near(line_rest)

    halves = links.meet(units(head, mark, weights, True, []))
    cross_keep, cross_send = units([cross_rest, cross_other], mark, weights, True, [halves[1][1]])
    lines_done = []

    def second_waits(odd):
        cross_come = links.near(hold([cross_send], [odd])[0])
        parts = fold(cross_keep, [cross_come], lines, [])
        lines_done.extend([odd, parts])
        lines_done.extend(units([line_rest, line_other], mark, weights, True, [odd]))
        return [lines_done[2]]

    held = links.meet_line(halves, [cross_keep], second_waits)
    odd, cross_parts, line_keep, line_send = lines_done
    come = links.line(held, bits[0])
    line_come = links.near(hold([line_send], [held])[0])
    sums = [held, come]
    if subs > 1:
        come = jnp.concatenate([come[chunk:], come[:chunk]], axis=0)
        sums = [lax.psum(held.astype(F32) + come.astype(F32), "sub")]
    line_parts = fold(line_keep, [line_come], lines, [])

    blocks = {}
    for place in reversed(range(lines)):
        blocks[offsets[place]] = [line_parts[place], links.far(cross_parts[place])]
    summed = {}
    for bit in reversed(bits):
        for offset in reversed(offsets):
            if offset & bit and offset < 2 * bit * (lines // bit) and not offset & (bit - 1):
                summed[offset] = add(blocks[offset])
                blocks[offset ^ bit].append(links.line(summed[offset], bit))
    rest_terms = blocks[0]
    features, draft_in = mid(hid, hid_beside, sums, draft_gain.reshape(1, width), [summed[lines - 1]])
    a_lined = [draft_in]
    for bit in bits[1:]:
        a_lined = a_lined + [links.line(block, bit) for block in a_lined]
    a_crossed = [links.far(block) for block in a_lined]
    own = [pack(a_lined, [blocks[lines // 2][1]]), pack(a_crossed, [summed[1], summed[lines // 2]])]
    pieces = own + [links.near(piece) for piece in own]
    halves = links.meet(units(pieces, mark, draft_weights, False, []))
    held = links.meet_line(halves, [], lambda odd: [blocks[0][1], blocks[0][2]])
    keep, send = add([held], [], 2)
    terms = [keep, links.line(send, bits[0])]

    draft_out = last(features, terms, final_gain.reshape(1, width), requests, rounds)
    verified = merge(
        accepted,
        [[features], [rest_hid] + over_sub(rest_terms)],
        rows,
        rounds,
    )
    return verified.transpose(1, 0, 2), draft_out


def solution(mesh):
    placed = (
        P(None, ("groups", "expert", "tensor"), None),
        P(None, ("groups", "expert", "tensor"), None),
        P(None, ("groups", "expert", "tensor")),
        P(),
        P(),
        P(("expert", "tensor"), None, "sub"),
        P(("expert", "tensor"), None, "sub"),
        P(("expert", "tensor"), "sub", None),
        P(),
        P(None, ("expert", "tensor")),
        P(None, ("expert", "tensor")),
        P(("expert", "tensor"), None),
        P(),
    )
    body = functools.partial(
        local, mesh.shape["expert"], mesh.shape["tensor"], mesh.shape["sub"]
    )
    return jax.shard_map(
        body,
        mesh=mesh,
        in_specs=placed,
        out_specs=(
            P(None, ("groups", "expert", "tensor"), None),
            P(None, ("groups", "expert", "tensor"), None),
        ),
        check_vma=False,
    )
```
